512 devices in a mesh: seq: 128 (over y, z_lo, x), mp: 4 (over z_hi, core).
Axes of the slice: x: 4, y: 8, z: 8 (z_hi: 2, z_lo: 4; z = z_hi * 4 + z_lo), core: 2. Of those that a mesh axis runs over, the one named last changes fastest.
Arguments:
- state: bfloat16 [61440, 1024], P('seq'), may hold values from -60 to 60
- condition: bfloat16 [61440, 1024], P('seq'), may hold values from -6 to 6
- time_vector: bfloat16 [1024], replicated, may hold values from -4 to 4
- norm_gain: bfloat16 [1024], replicated, may hold values from 0.59765625 to 1.3984375
- w_qkv: bfloat16 [3, 1024, 1024], P(None, None, 'mp'), may hold values from -2 to 2
- w_out: bfloat16 [1024, 1024], P('mp'), may hold values from -0.75 to 0.75
- utterance_ids: int32 [61440], P('seq'), may hold values from 0 to 239, never falling along the last dimension, each value on 1 to 1024 neighbouring positions
Outputs:
- final_state: bfloat16 [61440, 1024], P('seq', 'mp')
The draws below stay inside these ranges and needn't reach their ends.
Inputs may be any that keep to these rules, and one draw needn't show every extreme that they name: `utterance_ids`: never falling along the frames; each utterance has 1 to 1024 frames and one has exactly 1024.
All inputs are finite; a program needn't handle non-finite values.
Results may differ from the reference program's by a relative error of at most 0.03.
Values may be sent and summed in bfloat16 or wider, within the bound.
A program may use at most 64 MiB of HBM per device.

```python
import math
import jax
import jax.numpy as jnp
import numpy as np
from jax import lax

D = 1024
HEAD_DIM = 64
BLOCK = 24
MAX_LEN = 1024
FRAMES = 61440
UTTS = 240


def draw_state(key, part):
    key = jax.random.fold_in(key, 11)
    values = jnp.clip(jax.random.normal(key, (FRAMES, D), jnp.float32), -6.0, 6.0)
    return values.astype(jnp.bfloat16)


def draw_w_qkv(key, part):
    key = jax.random.fold_in(key, 12)
    factors = jnp.array([4.0, 1.0, 1.0], jnp.float32)[:, None, None] * D ** (-0.5)
    weights = jnp.clip(jax.random.normal(key, (3, D, D), jnp.float32), -5.0, 5.0) * factors
    return weights.astype(jnp.bfloat16)


def block_scale(key, dims, shards, low, high):
    def one(dim, blocks):
        draws = jax.random.uniform(jax.random.fold_in(jax.random.fold_in(key, 6), dim), (blocks,), jnp.float32, low / len(shards), high / len(shards))
        return jnp.repeat(jnp.exp(draws), dims[dim] // blocks).reshape((-1,) + (1,) * (len(dims) - dim - 1))

    loudness = one(*shards[0])
    for cut in shards[1:]:
        loudness = loudness * one(*cut)
    return loudness


def split_up(count, total, most, lean):
    portions = [(1 << 20) // math.isqrt(grade ** lean) + 1 for grade in range(2, count + 1)]
    rest, holding = total - most - (count - 1), [1] * (count - 1)
    while rest > 0:
        candidates = [i for i in range(count - 1) if holding[i] < most]
        pool, left = sum([portions[i] for i in candidates]), rest
        for i in candidates:
            addition = min(most - holding[i], max(1, left * portions[i] // pool), rest)
            holding[i] = holding[i] + addition
            rest = rest - addition
    return np.array([most] + holding)


def ragged_sizes(key, count, total, limit, slope):
    if count == 2:
        one = jax.random.randint(key, (), max(1, total - limit), min(limit, total - 1) + 1)
        return jnp.stack([one, total - one])
    sizes = jnp.asarray(split_up(count, total, limit, slope), jnp.int32)
    pairs = (count - 1) // 2
    giver, taker = sizes[1:1 + 2 * pairs:2], sizes[2:2 + 2 * pairs:2]
    room = jnp.minimum(giver - 1, limit - taker)
    moved = jax.random.randint(jax.random.fold_in(key, 1), (pairs,), 0, 1 << 20) % (room + 1)
    sizes = sizes.at[1:1 + 2 * pairs:2].set(giver - moved).at[2:2 + 2 * pairs:2].set(taker + moved)
    return sizes[jax.random.permutation(jax.random.fold_in(key, 2), count)]


def bell_draw(rng, dims, deviation, reach, pieces=(), kind=jnp.bfloat16):
    values = deviation * jax.random.normal(rng, dims, jnp.float32)
    if pieces:
        values = values * block_scale(rng, dims, pieces, -0.22, 0.18)
    return jnp.clip(values, -reach, reach).astype(kind)


def setup_inputs(seed: int = 0) -> dict:
    key_list = jax.random.split(jax.random.key(seed), 8)
    return {
        "state": draw_state(jax.random.fold_in(key_list[7], 71), 0),
        "condition": bell_draw(key_list[1], (FRAMES, D), 1.0, 6.0, ((0, 128),)),
        "time_vector": bell_draw(key_list[2], (D,), 1.0, 4.0),
        "norm_gain": jnp.clip(1.0 + 0.08 * jax.random.normal(key_list[3], (D,), jnp.float32), 0.59765625, 1.3984375).astype(jnp.bfloat16),
        "w_qkv": draw_w_qkv(jax.random.fold_in(key_list[7], 71), 0),
        "w_out": bell_draw(key_list[5], (D, D), (D // 16) ** -0.5, 0.75, ((0, 4),)),
        "utterance_ids": jnp.searchsorted(jnp.cumsum(ragged_sizes(key_list[6], UTTS, FRAMES, MAX_LEN, 2)), jnp.arange(FRAMES), side="right").astype(jnp.int32),
    }


def attend_all(q, k, v, seg_plus):
    padded_k = jnp.pad(k, ((2 * BLOCK, BLOCK), (0, 0)))
    padded_v = jnp.pad(v, ((2 * BLOCK, BLOCK), (0, 0)))
    padded_s = jnp.pad(seg_plus, (2 * BLOCK, BLOCK))
    heads = D // HEAD_DIM

    def one_block(index):
        start = (index * BLOCK).astype(jnp.int32)
        q_rows = lax.dynamic_slice_in_dim(q, start, BLOCK, 0).reshape(BLOCK, heads, HEAD_DIM)
        k_rows = lax.dynamic_slice_in_dim(padded_k, start, 4 * BLOCK, 0).reshape(4 * BLOCK, heads, HEAD_DIM)
        v_rows = lax.dynamic_slice_in_dim(padded_v, start, 4 * BLOCK, 0).reshape(4 * BLOCK, heads, HEAD_DIM)
        q_seg = lax.dynamic_slice_in_dim(seg_plus, start, BLOCK, 0)
        k_seg = lax.dynamic_slice_in_dim(padded_s, start, 4 * BLOCK, 0)
        scores = jnp.einsum('qhe,khe->hqk', q_rows.astype(jnp.float32), k_rows.astype(jnp.float32)) * 0.125
        allowed = (q_seg[:, None] == k_seg[None, :])[None]
        scores = jnp.where(allowed, scores, -1e+30)
        top = lax.optimization_barrier(jnp.max(scores, axis=-1, keepdims=True))
        expo = jnp.exp(scores - top)
        probs = (expo / lax.optimization_barrier(jnp.sum(expo, axis=-1, keepdims=True))).astype(jnp.bfloat16)
        out = jnp.einsum('hqk,khe->qhe', probs.astype(jnp.float32), v_rows.astype(jnp.float32))
        return out.astype(jnp.bfloat16).reshape(BLOCK, D)
    blocks = lax.map(one_block, jnp.arange(FRAMES // BLOCK, dtype=jnp.int32))
    return blocks.reshape(FRAMES, D)

def reference(state, condition, time_vector, norm_gain, w_qkv, w_out, utterance_ids):
    x = state.astype(jnp.float32)
    seg_plus = utterance_ids + 1
    for step in range(2):
        t = 0.5 * step
        h = x + condition.astype(jnp.float32) + t * time_vector.astype(jnp.float32)
        scale = lax.rsqrt(lax.optimization_barrier(jnp.mean(h * h, axis=-1, keepdims=True)) + 1e-06)
        normed = (h * scale * norm_gain.astype(jnp.float32)).astype(jnp.bfloat16)
        q = jnp.dot(normed, w_qkv[0], preferred_element_type=jnp.float32).astype(jnp.bfloat16)
        k = jnp.dot(normed, w_qkv[1], preferred_element_type=jnp.float32).astype(jnp.bfloat16)
        v = jnp.dot(normed, w_qkv[2], preferred_element_type=jnp.float32).astype(jnp.bfloat16)
        attended = attend_all(q, k, v, seg_plus)
        velocity = jnp.dot(attended, w_out, preferred_element_type=jnp.float32)
        x = x + 0.5 * velocity
    return x.astype(jnp.bfloat16)
```

```python
import jax
import jax.numpy as jnp
from jax import lax
from jax.experimental import pallas as pl
from jax.experimental.pallas import tpu as pltpu
from jax.sharding import PartitionSpec as P

MESH = pl.DeviceIdType.MESH
BF16 = jnp.bfloat16
F32 = jnp.float32

D = 1024
BLOCK = 24
ROWS = 480
EXT = 560
OWN = 48
TILE = 48
KEYS = 128
TILES = ROWS // TILE
LANES = 640
CHUNK = 96
CHUNKS = ROWS // CHUNK
BOUNDARY_FIRST = (0, CHUNKS - 1) + tuple(range(1, CHUNKS - 1))
PARTS = 8


def kernel(
    state_h, cond_h, wqkv_h, wout_h, tvec, gain, ids, out,
    st, cd, wq, wo, fq, fo, n1, n2, ids_prev, ids_next, bias, qa, qb, k, v, att, acc,
    pv_out, pv_in, x1, fin_out, fin_in,
    load_sem, zs, zr, xs, xr, ys, yr, hs, hr, ds, dr,
):
    seq = lax.axis_index("seq")
    mp = lax.axis_index("mp")
    x = seq % 4
    y = seq // 16
    odd = y % 2
    zh = mp // 2
    core = mp % 2
    part = x + 4 * odd

    at_z = (seq, (1 - zh) * 2 + core)
    at_x = [(seq - x + (x + hop) % 4, mp) for hop in (1, 2, 3)]
    sides = [1 - 2 * odd, 2 * odd - 1]
    at_y = [((seq + 16 * side + 128) % 128, mp) for side in sides]
    before = ((seq + 127) % 128, mp)
    after = ((seq + 1) % 128, mp)
    twin = (seq, zh * 2 + 1 - core)

    barrier = pltpu.get_barrier_semaphore()
    partners = [at_z] + at_x + at_y + [before, after, twin]
    for device in partners:
        pl.semaphore_signal(barrier, inc=1, device_id=device, device_id_type=MESH)

    loads = [
        pltpu.make_async_copy(src, dst, load_sem.at[i])
        for i, (src, dst) in enumerate(((state_h, st), (cond_h, cd), (wqkv_h, wq), (wout_h, wo)))
    ]
    for load in loads:
        load.start()

    def remote(src, dst, send, recv, device):
        return pltpu.make_async_remote_copy(
            src_ref=src, dst_ref=dst, send_sem=send, recv_sem=recv, device_id=device, device_id_type=MESH
        )

    def piece(pair, s, first, count=1):
        if s < 6:
            return pair[0].at[s // 2, pl.ds(512 * (s % 2) + 64 * first, 64 * count)]
        return pair[1].at[pl.ds(128 * (s % 2) + 16 * first, 16 * count)]

    mine, foreign = (wq, wo), (fq, fo)

    def z_copy(s):
        return remote(piece(mine, s, part), piece(foreign, s, part), zs.at[s], zr.at[s], at_z)

    def x_copy(s, hop):
        i = 3 * s + hop
        return remote(piece(foreign, s, part), piece(foreign, s, part), xs.at[i], xr.at[i], at_x[hop])

    def x_arrival(s, hop):
        other = (x + 3 - hop) % 4 + 4 * odd
        i = 3 * s + hop
        return remote(piece(foreign, s, other), piece(foreign, s, other), xs.at[i], xr.at[i], at_x[hop])

    def y_copy(s):
        block = piece(foreign, s, 4 * odd, 4)
        return remote(block, block, ys.at[s], yr.at[s], at_y[s % 2])

    def y_arrival(s):
        block = piece(foreign, s, 4 * (1 - odd), 4)
        return remote(block, block, ys.at[s], yr.at[s], at_y[s % 2])

    def tick_z(s):
        z_copy(s).wait_recv()
        for hop in range(3):
            x_copy(s, hop).start()

    def tick_x(s):
        for hop in range(3):
            x_arrival(s, hop).wait_recv()
        y_copy(s).start()

    def tick_y(s):
        y_arrival(s).wait_recv()

    def halo_copies(n, base):
        return (
            remote(n.at[pl.ds(OWN + ROWS - 48, 48)], n.at[pl.ds(0, 48)], hs.at[base], hr.at[base], after),
            remote(n.at[pl.ds(OWN, 32)], n.at[pl.ds(OWN + ROWS, 32)], hs.at[base + 1], hr.at[base + 1], before),
        )

    id_copies = (
        remote(ids, ids_prev, hs.at[4], hr.at[4], after),
        remote(ids, ids_next, hs.at[5], hr.at[5], before),
    )

    def normalise(h, n, r0, rows):
        scale = lax.rsqrt(jnp.mean(h * h, axis=1, keepdims=True) + 1e-06)
        n[pl.ds(OWN + r0, rows), :] = (h * scale * gain[...].astype(F32)).astype(BF16)

    loads[0].wait()
    loads[1].wait()

    def first_norm(i, _):
        r0 = pl.multiple_of(i * 48, 48)
        h = st[pl.ds(r0, 48), :].astype(F32) + cd[pl.ds(r0, 48), :].astype(F32)
        normalise(h, n1, r0, 48)
        return 0

    lax.fori_loop(0, ROWS // 48, first_norm, 0)
    loads[2].wait()
    loads[3].wait()

    pl.semaphore_wait(barrier, len(partners))
    for s in range(PARTS):
        z_copy(s).start()
    first_halo = halo_copies(n1, 0)
    for copy in first_halo + id_copies:
        copy.start()

    for p in range(4):
        v[:, 256 * p + 128 : 256 * p + 256] = jnp.ones((EXT, 128), BF16)

    low = lax.broadcasted_iota(jnp.int32, (1, 128), 1) < 64

    def queries(n, w, pair):
        r = jnp.dot(n[OWN : OWN + ROWS, :], w[0], preferred_element_type=F32) * 0.125
        zero = jnp.zeros((), BF16)
        for j in range(2):
            c = 128 * (pair + j)
            part_q = r[:, 128 * j : 128 * j + 128].astype(BF16)
            qa[:, c : c + 128] = jnp.where(low, part_q, zero)
            qb[:, c : c + 128] = jnp.where(low, zero, part_q)

    def keys(n, w, pair, r0, rows):
        r = jnp.dot(n[r0 : r0 + rows, :], w[1], preferred_element_type=F32)
        k[r0 : r0 + rows, 128 * pair : 128 * pair + 256] = r.astype(BF16)

    def values(n, w, pair, r0, rows):
        r = jnp.dot(n[r0 : r0 + rows, :], w[2], preferred_element_type=F32).astype(BF16)
        for j in range(2):
            c = 256 * (pair + j)
            v[r0 : r0 + rows, c : c + 128] = r[:, 128 * j : 128 * j + 128]

    def build_bias():
        lane = lax.broadcasted_iota(jnp.int32, (8, LANES), 1)
        ext = jnp.where(
            lane < OWN,
            jnp.where(seq == 0, -1.0, pltpu.roll(ids_prev[...], LANES - (ROWS - 48), 1)),
            jnp.where(
                lane < OWN + ROWS,
                pltpu.roll(ids[...], OWN, 1),
                jnp.where(seq == 127, -2.0, pltpu.roll(ids_next[...], OWN + ROWS, 1)),
            ),
        )
        row = lax.broadcasted_iota(jnp.int32, (TILE, KEYS), 0)
        col = lax.broadcasted_iota(jnp.int32, (TILE, KEYS), 1)
        first = jnp.where(row < BLOCK, 0, BLOCK)
        window = (col >= first) & (col < first + 4 * BLOCK)
        for t in range(TILES):
            moved = ext if t == 0 else pltpu.roll(ext, LANES - TILE * t, 1)
            key_ids = jnp.broadcast_to(moved[0:1, :KEYS], (TILE, KEYS))
            query_ids = jnp.sum(jnp.where(col == row + OWN, key_ids, 0.0), axis=1, keepdims=True)
            bias[TILE * t : TILE * t + TILE, :] = jnp.where(window & (query_ids == key_ids), 0.0, -1e30)

    def attend(r0, pairs):
        b = bias[pl.ds(r0, TILE), :]
        b2 = jnp.concatenate([b, b], axis=0)
        for p in pairs:
            c = 128 * p
            q2 = jnp.concatenate([qa[pl.ds(r0, TILE), c : c + 128], qb[pl.ds(r0, TILE), c : c + 128]], axis=0)
            scores = lax.dot_general(
                q2, k[pl.ds(r0, KEYS), c : c + 128], (((1,), (1,)), ((), ())), preferred_element_type=F32
            )
            scores = scores + b2
            e = jnp.exp(scores - jnp.max(scores, axis=1, keepdims=True)).astype(BF16)
            o = jnp.dot(e, v[pl.ds(r0, KEYS), 2 * c : 2 * c + 256], preferred_element_type=F32)
            num = jnp.where(low, o[:TILE, :128], o[TILE:, :128])
            den = jnp.where(low, o[:TILE, 128:], o[TILE:, 128:])
            att[pl.ds(r0, TILE), c : c + 128] = (num / den).astype(BF16)

    def attend_some(tiles, pairs):
        start, stop = tiles

        def body(i, _):
            for j in range(2):
                attend(pl.multiple_of((start + 2 * i + j) * TILE, TILE), pairs)
            return 0

        lax.fori_loop(0, (stop - start) // 2, body, 0)

    queries(n1, wq, 0)
    for copy in first_halo + id_copies:
        copy.wait_recv()
    keys(n1, wq, 0, 0, EXT)
    values(n1, wq, 0, 0, EXT)
    tick_z(0)
    build_bias()
    attend_some((0, 4), (0, 1))
    tick_z(1)
    attend_some((4, 10), (0, 1))
    tick_z(2)
    tick_x(0)
    for c in range(0, D, 512):
        acc[:, c : c + 512] = jnp.dot(att[:, :256], wo[:, c : c + 512], preferred_element_type=F32)
    tick_z(3)
    tick_x(1)
    tick_z(4)
    tick_x(2)
    tick_y(0)
    tick_z(5)
    tick_x(3)
    tick_y(1)
    queries(n1, fq, 2)
    tick_z(6)
    tick_x(4)
    tick_y(2)
    tick_z(7)
    tick_x(5)
    tick_y(3)
    keys(n1, fq, 2, 0, EXT)
    tick_x(6)
    tick_y(4)
    tick_x(7)
    tick_y(5)
    values(n1, fq, 2, 0, EXT)
    attend_some((0, TILES), (2, 3))
    tick_y(6)
    tick_y(7)

    def pv_copy(r):
        rows = pl.ds(CHUNK * r, CHUNK)
        return remote(pv_out.at[rows], pv_in.at[rows], ds.at[r], dr.at[r], twin)

    for r in BOUNDARY_FIRST:
        rows = slice(CHUNK * r, CHUNK * r + CHUNK)
        total = acc[rows, :] + jnp.dot(att[rows, 256:512], fo[...], preferred_element_type=F32)
        acc[rows, :] = total
        pv_out[rows, :] = total.astype(BF16)
        pv_copy(r).start()

    second_halo = halo_copies(n2, 2)
    for r in BOUNDARY_FIRST:
        pv_copy(r).wait_recv()
        for r0 in range(CHUNK * r, CHUNK * r + CHUNK, 48):
            rows = slice(r0, r0 + 48)
            x_new = st[rows, :].astype(F32) + 0.5 * (acc[rows, :] + pv_in[rows, :].astype(F32))
            x1[rows, :] = x_new
            h = x_new + cd[rows, :].astype(F32) + 0.5 * tvec[...].astype(F32)
            normalise(h, n2, r0, 48)
        if r == 0:
            second_halo[1].start()
        if r == CHUNKS - 1:
            second_halo[0].start()

    for w, pair in ((wq, 0), (fq, 2)):
        queries(n2, w, pair)
        keys(n2, w, pair, OWN, ROWS)
        values(n2, w, pair, OWN, ROWS)
    attend_some((1, 9), range(4))
    for copy in second_halo:
        copy.wait_recv()
    for w, pair in ((wq, 0), (fq, 2)):
        for r0, rows in ((0, OWN), (OWN + ROWS, 32)):
            keys(n2, w, pair, r0, rows)
            values(n2, w, pair, r0, rows)
    attend(0, range(4))
    attend((TILES - 1) * TILE, range(4))

    my_cols = pl.ds(pl.multiple_of(512 * zh + 256 * core, 256), 256)
    twin_cols = pl.ds(pl.multiple_of(512 * zh + 256 * (1 - core), 256), 256)

    def terms(cols):
        return jnp.dot(att[:, :256], wo[:, cols], preferred_element_type=F32) + jnp.dot(
            att[:, 256:512], fo[:, cols], preferred_element_type=F32
        )

    fin_out[...] = terms(twin_cols).astype(BF16)
    fin_copy = remote(fin_out, fin_in, ds.at[CHUNKS], dr.at[CHUNKS], twin)
    fin_copy.start()
    acc[:, 0:256] = x1[:, my_cols] + 0.5 * terms(my_cols)
    fin_copy.wait_recv()
    out[...] = (acc[:, 0:256] + 0.5 * fin_in[...].astype(F32)).astype(BF16)

    for s in range(PARTS):
        z_copy(s).wait_send()
        for hop in range(3):
            x_copy(s, hop).wait_send()
        y_copy(s).wait_send()
    for copy in first_halo + id_copies + second_halo:
        copy.wait_send()
    for r in range(CHUNKS):
        pv_copy(r).wait_send()
    fin_copy.wait_send()


def shards(state, condition, time_vector, norm_gain, w_qkv, w_out, utterance_ids):
    ids = jnp.broadcast_to(jnp.pad(utterance_ids.astype(F32), (0, LANES - ROWS)), (8, LANES))
    any_spec = pl.BlockSpec(memory_space=pl.ANY)
    vmem = pl.BlockSpec(memory_space=pltpu.VMEM)
    dma = pltpu.SemaphoreType.DMA
    return pl.pallas_call(
        kernel,
        out_shape=jax.ShapeDtypeStruct((ROWS, 256), BF16),
        in_specs=[any_spec] * 4 + [vmem] * 3,
        out_specs=vmem,
        scratch_shapes=[
            pltpu.VMEM((ROWS, D), BF16),
            pltpu.VMEM((ROWS, D), BF16),
            pltpu.VMEM((3, D, 256), BF16),
            pltpu.VMEM((256, D), BF16),
            pltpu.VMEM((3, D, 256), BF16),
            pltpu.VMEM((256, D), BF16),
            pltpu.VMEM((EXT, D), BF16),
            pltpu.VMEM((EXT, D), BF16),
            pltpu.VMEM((8, LANES), F32),
            pltpu.VMEM((8, LANES), F32),
            pltpu.VMEM((ROWS, KEYS), F32),
            pltpu.VMEM((ROWS, 512), BF16),
            pltpu.VMEM((ROWS, 512), BF16),
            pltpu.VMEM((EXT, 512), BF16),
            pltpu.VMEM((EXT, 1024), BF16),
            pltpu.VMEM((ROWS, 512), BF16),
            pltpu.VMEM((ROWS, D), F32),
            pltpu.VMEM((ROWS, D), BF16),
            pltpu.VMEM((ROWS, D), BF16),
            pltpu.VMEM((ROWS, D), F32),
            pltpu.VMEM((ROWS, 256), BF16),
            pltpu.VMEM((ROWS, 256), BF16),
            dma((4,)),
            dma((PARTS,)),
            dma((PARTS,)),
            dma((3 * PARTS,)),
            dma((3 * PARTS,)),
            dma((PARTS,)),
            dma((PARTS,)),
            dma((6,)),
            dma((6,)),
            dma((CHUNKS + 1,)),
            dma((CHUNKS + 1,)),
        ],
        compiler_params=pltpu.CompilerParams(
            collective_id=0, has_side_effects=True, vmem_limit_bytes=48 << 20
        ),
        cost_estimate=pl.CostEstimate(flops=4_500_000_000, bytes_accessed=4_500_000, transcendentals=1_500_000),
        name="decoder",
    )(state, condition, w_qkv, w_out, time_vector.reshape(1, D), norm_gain.reshape(1, D), ids)


def solution(mesh):
    in_specs = (
        P("seq", None),
        P("seq", None),
        P(),
        P(),
        P(None, None, "mp"),
        P("mp", None),
        P("seq"),
    )
    out_specs = P("seq", "mp")
    return jax.shard_map(shards, mesh=mesh, in_specs=in_specs, out_specs=out_specs, check_vma=False)
```

```python
import jax
import jax.numpy as jnp
from jax import lax
from jax.experimental import pallas as pl
from jax.experimental.pallas import tpu as pltpu
from jax.sharding import PartitionSpec as P

MESH = pl.DeviceIdType.MESH
BF16 = jnp.bfloat16
F32 = jnp.float32

D = 1024
BLOCK = 24
ROWS = 480
EXT = 560
OWN = 48
TILE = 48
KEYS = 128
TILES = ROWS // TILE
LANES = 640
CHUNK = 96
CHUNKS = ROWS // CHUNK
BOUNDARY_FIRST = (0, CHUNKS - 1) + tuple(range(1, CHUNKS - 1))
PARTS = 8


def kernel(
    state_h, cond_h, wqkv_h, wout_h, tvec_h, gain_h, ids_h, out,
    st, cd, wq, wo, fq, fo, tvec, gain, ids, n1, n2, h1, h2, ids_prev, ids_next, bias, qa, qb, k, v, att, acc,
    pv_out, pv_in, x1, fin_out, fin_in,
    load_sem, zs, zf, zr, xs, xr, ys, yr, hs, hr, ds, dr,
):
    seq = lax.axis_index("seq")
    mp = lax.axis_index("mp")
    x = seq % 4
    y = seq // 16
    odd = y % 2
    zh = mp // 2
    core = mp % 2
    colour = (x + 2 * odd) % 4

    zl = (seq // 4) % 4
    up = (jnp.where(zl == 3, seq - 12, seq + 4), jnp.where(zl == 3, 1 - zh, zh) * 2 + core)
    down = (jnp.where(zl == 0, seq + 12, seq - 4), jnp.where(zl == 0, 1 - zh, zh) * 2 + core)
    outer = (zl == 0) | (zl == 3)
    across = [jnp.where(zl == 3, a, b) for a, b in zip(up, down)]
    inward = [jnp.where(zl == 3, b, a) for a, b in zip(up, down)]
    at_x = [(seq - x + (x + hop) % 4, mp) for hop in (1, 3)]
    at_y = [((seq + 16 * hop) % 128, mp) for hop in (1, 7)]
    before = ((seq + 127) % 128, mp)
    after = ((seq + 1) % 128, mp)
    twin = (seq, zh * 2 + 1 - core)

    barrier = pltpu.get_barrier_semaphore()
    partners = [up, down] + at_x + at_y + [twin]
    for device in partners:
        pl.semaphore_signal(barrier, inc=1, device_id=device, device_id_type=MESH)

    has_before = seq > 0
    has_after = seq < 127

    @pl.when(has_before)
    def _():
        pl.semaphore_signal(barrier, inc=1, device_id=before, device_id_type=MESH)

    @pl.when(has_after)
    def _():
        pl.semaphore_signal(barrier, inc=1, device_id=after, device_id_type=MESH)

    loads = [
        pltpu.make_async_copy(src, dst, load_sem.at[i])
        for i, (src, dst) in enumerate(
            (
                (gain_h, gain),
                (state_h, st),
                (cond_h, cd),
                (ids_h, ids),
                (wqkv_h, wq),
                (wout_h, wo),
                (tvec_h, tvec),
            )
        )
    ]
    for load in loads:
        load.start()

    def remote(src, dst, send, recv, device):
        return pltpu.make_async_remote_copy(
            src_ref=src, dst_ref=dst, send_sem=send, recv_sem=recv, device_id=device, device_id_type=MESH
        )

    def piece(pair, s, which, half=None):
        size, ref = (128, pair[0].at[s // 2]) if s < 6 else (32, pair[1])
        first = 4 * size * (s % 2) + size * which
        if half is not None:
            size = size // 2
            first = first + size * half
        return ref.at[pl.ds(pl.multiple_of(first, 16), size)]

    mine, foreign = (wqkv_h, wout_h), (fq, fo)

    def z_copy(s):
        return remote(piece(mine, s, colour), piece(foreign, s, colour), zs.at[s], zr.at[s], across)

    def z_forward(s):
        return remote(piece(foreign, s, colour), piece(foreign, s, colour), zf.at[s], zr.at[s], inward)

    def x_copy(s, j, which):
        i = 2 * s + j
        return remote(piece(foreign, s, which), piece(foreign, s, which), xs.at[i], xr.at[i], at_x[j])

    def y_copy(s, j, which):
        i = 2 * s + j
        return remote(piece(foreign, s, which, j), piece(foreign, s, which, j), ys.at[i], yr.at[i], at_y[j])

    def tick(s):
        z_copy(s).wait_recv()

        @pl.when(outer)
        def _():
            z_forward(s).start()

        for j in range(2):
            x_copy(s, j, colour).start()
            y_copy(s, j, colour).start()

    def complete(s):
        for j in range(2):
            x_copy(s, j, (colour + 3 - 2 * j) % 4).wait_recv()
            y_copy(s, j, (colour + 2) % 4).wait_recv()

    def halo_copies(n, h, base):
        return (
            remote(n.at[pl.ds(ROWS - 48, 48)], h.at[pl.ds(0, 48)], hs.at[base], hr.at[base], after),
            remote(n.at[pl.ds(0, 32)], h.at[pl.ds(48, 32)], hs.at[base + 1], hr.at[base + 1], before),
        )

    id_copies = (
        remote(ids, ids_prev, hs.at[4], hr.at[4], after),
        remote(ids, ids_next, hs.at[5], hr.at[5], before),
    )

    def send_after(copies):
        @pl.when(has_after)
        def _():
            for copy in copies:
                copy.start()

    def send_before(copies):
        @pl.when(has_before)
        def _():
            for copy in copies:
                copy.start()

    def halo_arrived(copies):
        @pl.when(has_before)
        def _():
            for copy in copies[::2]:
                copy.wait_recv()

        @pl.when(has_after)
        def _():
            for copy in copies[1::2]:
                copy.wait_recv()

    def halo_left(copies):
        @pl.when(has_after)
        def _():
            for copy in copies[::2]:
                copy.wait_send()

        @pl.when(has_before)
        def _():
            for copy in copies[1::2]:
                copy.wait_send()

    def normalise(h, n, r0, rows):
        scale = lax.rsqrt(jnp.mean(h * h, axis=1, keepdims=True) + 1e-06)
        n[pl.ds(r0, rows), :] = (h * scale * gain[...].reshape(1, D).astype(F32)).astype(BF16)

    pl.semaphore_wait(barrier, len(partners) + jnp.where(has_before & has_after, 2, 1))

    @pl.when(outer)
    def _():
        for s in range(PARTS):
            z_copy(s).start()

    for load in loads[:4]:
        load.wait()

    def first_norm(i, _):
        r0 = pl.multiple_of(i * 48, 48)
        h = st[pl.ds(r0, 48), :].astype(F32) + cd[pl.ds(r0, 48), :].astype(F32)
        normalise(h, n1, r0, 48)
        return 0

    lax.fori_loop(0, ROWS // 48, first_norm, 0)
    first_halo = halo_copies(n1, h1, 0)
    send_after((first_halo[0], id_copies[0]))
    send_before((first_halo[1], id_copies[1]))

    @pl.when(seq == 0)
    def _():
        for h in (h1, h2):
            h[0:48, :] = jnp.zeros((48, D), BF16)

    @pl.when(seq == 127)
    def _():
        for h in (h1, h2):
            h[48:80, :] = jnp.zeros((32, D), BF16)

    for load in loads[4:]:
        load.wait()

    for p in range(4):
        v[:, 256 * p + 128 : 256 * p + 256] = jnp.ones((EXT, 128), BF16)

    low = lax.broadcasted_iota(jnp.int32, (1, 128), 1) < 64

    def queries(n, w, pair):
        r = jnp.dot(n[...], w[0], preferred_element_type=F32) * 0.125
        zero = jnp.zeros((), BF16)
        for j in range(2):
            c = 128 * (pair + j)
            part_q = r[:, 128 * j : 128 * j + 128].astype(BF16)
            qa[:, c : c + 128] = jnp.where(low, part_q, zero)
            qb[:, c : c + 128] = jnp.where(low, zero, part_q)

    def spans(halo):
        return ((0, 0, 48), (48, OWN + ROWS, 32)) if halo else ((0, OWN, ROWS),)

    def keys(n, w, pair, halo=False):
        r = jnp.dot(n[...], w[1], preferred_element_type=F32).astype(BF16)
        for r0, to, rows in spans(halo):
            k[to : to + rows, 128 * pair : 128 * pair + 256] = r[r0 : r0 + rows]

    def values(n, w, pair, halo=False):
        r = jnp.dot(n[...], w[2], preferred_element_type=F32).astype(BF16)
        for r0, to, rows in spans(halo):
            for j in range(2):
                c = 256 * (pair + j)
                v[to : to + rows, c : c + 128] = r[r0 : r0 + rows, 128 * j : 128 * j + 128]

    def build_bias():
        lane = lax.broadcasted_iota(jnp.int32, (8, LANES), 1)

        def wide(ref):
            flat = ref[...].astype(F32).reshape(1, ROWS)
            flat = jnp.concatenate([flat, jnp.zeros((1, LANES - ROWS), F32)], axis=1)
            return jnp.broadcast_to(flat, (8, LANES))

        ext = jnp.where(
            lane < OWN,
            jnp.where(seq == 0, -1.0, pltpu.roll(wide(ids_prev), LANES - (ROWS - 48), 1)),
            jnp.where(
                lane < OWN + ROWS,
                pltpu.roll(wide(ids), OWN, 1),
                jnp.where(seq == 127, -2.0, pltpu.roll(wide(ids_next), OWN + ROWS, 1)),
            ),
        )
        row = lax.broadcasted_iota(jnp.int32, (TILE, KEYS), 0)
        col = lax.broadcasted_iota(jnp.int32, (TILE, KEYS), 1)
        first = jnp.where(row < BLOCK, 0, BLOCK)
        window = (col >= first) & (col < first + 4 * BLOCK)
        for t in range(TILES):
            moved = ext if t == 0 else pltpu.roll(ext, LANES - TILE * t, 1)
            key_ids = jnp.broadcast_to(moved[0:1, :KEYS], (TILE, KEYS))
            query_ids = jnp.sum(jnp.where(col == row + OWN, key_ids, 0.0), axis=1, keepdims=True)
            bias[TILE * t : TILE * t + TILE, :] = jnp.where(window & (query_ids == key_ids), 0.0, -1e30)

    def attend(starts, pairs):
        scores = []
        for r0 in starts:
            b = bias[pl.ds(r0, TILE), :]
            b2 = jnp.concatenate([b, b], axis=0)
            for p in pairs:
                c = 128 * p
                q2 = jnp.concatenate([qa[pl.ds(r0, TILE), c : c + 128], qb[pl.ds(r0, TILE), c : c + 128]], axis=0)
                scores.append(
                    lax.dot_general(
                        q2, k[pl.ds(r0, KEYS), c : c + 128], (((1,), (1,)), ((), ())), preferred_element_type=F32
                    )
                    + b2
                )
        tops = [jnp.max(score, axis=1, keepdims=True) for score in scores]
        exps = [jnp.exp(score - top).astype(BF16) for score, top in zip(scores, tops)]
        where = [(r0, 128 * p) for r0 in starts for p in pairs]
        sums = [
            jnp.dot(e, v[pl.ds(r0, KEYS), 2 * c : 2 * c + 256], preferred_element_type=F32)
            for e, (r0, c) in zip(exps, where)
        ]
        for o, (r0, c) in zip(sums, where):
            num = jnp.where(low, o[:TILE, :128], o[TILE:, :128])
            den = jnp.where(low, o[:TILE, 128:], o[TILE:, 128:])
            att[pl.ds(r0, TILE), c : c + 128] = (num / den).astype(BF16)

    def attend_some(start, count, groups, pairs):
        def body(i, _):
            attend([pl.multiple_of((start + count * i + j) * TILE, TILE) for j in range(count)], pairs)
            return 0

        lax.fori_loop(0, groups, body, 0)

    queries(n1, wq, 0)
    tick(0)
    keys(n1, wq, 0)
    tick(1)
    values(n1, wq, 0)
    tick(2)
    tick(3)
    tick(4)
    halo_arrived(first_halo + id_copies)
    keys(h1, wq, 0, True)
    values(h1, wq, 0, True)
    build_bias()
    tick(5)
    attend_some(0, 5, 1, (0, 1))
    tick(6)
    attend_some(5, 5, 1, (0, 1))
    tick(7)
    complete(0)
    complete(1)
    queries(n1, fq, 2)
    for c in range(0, D, 512):
        acc[:, c : c + 512] = jnp.dot(att[:, :256], wo[:, c : c + 512], preferred_element_type=F32)
    complete(2)
    complete(3)
    keys(n1, fq, 2)
    keys(h1, fq, 2, True)
    complete(4)
    complete(5)
    values(n1, fq, 2)
    values(h1, fq, 2, True)
    attend_some(0, 5, 2, (2, 3))
    complete(6)
    complete(7)

    def pv_copy(r):
        rows = pl.ds(CHUNK * r, CHUNK)
        return remote(pv_out.at[rows], pv_in.at[rows], ds.at[r], dr.at[r], twin)

    for r in BOUNDARY_FIRST:
        rows = slice(CHUNK * r, CHUNK * r + CHUNK)
        total = acc[rows, :] + jnp.dot(att[rows, 256:512], fo[...], preferred_element_type=F32)
        acc[rows, :] = total
        pv_out[rows, :] = total.astype(BF16)
        pv_copy(r).start()

    second_halo = halo_copies(n2, h2, 2)
    for r in BOUNDARY_FIRST:
        pv_copy(r).wait_recv()
        for r0 in range(CHUNK * r, CHUNK * r + CHUNK, 48):
            rows = slice(r0, r0 + 48)
            x_new = st[rows, :].astype(F32) + 0.5 * (acc[rows, :] + pv_in[rows, :].astype(F32))
            x1[rows, :] = x_new
            h = x_new + cd[rows, :].astype(F32) + 0.5 * tvec[...].reshape(1, D).astype(F32)
            normalise(h, n2, r0, 48)
        if r == 0:
            send_before(second_halo[1:])
        if r == CHUNKS - 1:
            send_after(second_halo[:1])

    for w, pair in ((wq, 0), (fq, 2)):
        queries(n2, w, pair)
        keys(n2, w, pair)
        values(n2, w, pair)
    my_cols = pl.ds(pl.multiple_of(512 * zh + 256 * core, 256), 256)
    twin_cols = pl.ds(pl.multiple_of(512 * zh + 256 * (1 - core), 256), 256)

    def terms(r0, rows, cols):
        a = att[r0 : r0 + rows, :]
        return jnp.dot(a[:, :256], wo[:, cols], preferred_element_type=F32) + jnp.dot(
            a[:, 256:512], fo[:, cols], preferred_element_type=F32
        )

    INNER, FIRST, LAST = (TILE, ROWS - 2 * TILE), (0, TILE), (ROWS - TILE, TILE)

    def fin_copy(i, r0, rows):
        span = pl.ds(r0, rows)
        return remote(fin_out.at[span], fin_in.at[span], ds.at[CHUNKS + i], dr.at[CHUNKS + i], twin)

    def send_terms(i, r0, rows):
        fin_out[r0 : r0 + rows, :] = terms(r0, rows, twin_cols).astype(BF16)
        fin_copy(i, r0, rows).start()

    def finish(i, r0, rows):
        fin_copy(i, r0, rows).wait_recv()
        span = slice(r0, r0 + rows)
        out[span, :] = (acc[span, 0:256] + 0.5 * fin_in[span, :].astype(F32)).astype(BF16)

    def own_terms(r0, rows):
        acc[r0 : r0 + rows, 0:256] = x1[r0 : r0 + rows, my_cols] + 0.5 * terms(r0, rows, my_cols)

    attend_some(1, 4, 2, range(4))
    send_terms(0, *INNER)
    own_terms(*INNER)
    halo_arrived(second_halo)
    for w, pair in ((wq, 0), (fq, 2)):
        keys(h2, w, pair, True)
        values(h2, w, pair, True)
    attend((0, (TILES - 1) * TILE), range(4))
    send_terms(1, *FIRST)
    send_terms(2, *LAST)
    own_terms(*FIRST)
    own_terms(*LAST)
    for i, span in enumerate((INNER, FIRST, LAST)):
        finish(i, *span)

    for s in range(PARTS):


        @pl.when(outer)
        def _():
            z_copy(s).wait_send()
            z_forward(s).wait_send()

        for j in range(2):
            x_copy(s, j, colour).wait_send()
            y_copy(s, j, colour).wait_send()
    halo_left(first_halo + id_copies + second_halo)
    for r in range(CHUNKS):
        pv_copy(r).wait_send()
    for i, span in enumerate((INNER, FIRST, LAST)):
        fin_copy(i, *span).wait_send()


def shards(state, condition, time_vector, norm_gain, w_qkv, w_out, utterance_ids):
    any_spec = pl.BlockSpec(memory_space=pl.ANY)
    vmem = pl.BlockSpec(memory_space=pltpu.VMEM)
    dma = pltpu.SemaphoreType.DMA
    return pl.pallas_call(
        kernel,
        out_shape=jax.ShapeDtypeStruct((ROWS, 256), BF16),
        in_specs=[any_spec] * 7,
        out_specs=vmem,
        scratch_shapes=[
            pltpu.VMEM((ROWS, D), BF16),
            pltpu.VMEM((ROWS, D), BF16),
            pltpu.VMEM((3, D, 256), BF16),
            pltpu.VMEM((256, D), BF16),
            pltpu.VMEM((3, D, 256), BF16),
            pltpu.VMEM((256, D), BF16),
            pltpu.VMEM((D,), BF16),
            pltpu.VMEM((D,), BF16),
            pltpu.VMEM((ROWS,), jnp.int32),
            pltpu.VMEM((ROWS, D), BF16),
            pltpu.VMEM((ROWS, D), BF16),
            pltpu.VMEM((80, D), BF16),
            pltpu.VMEM((80, D), BF16),
            pltpu.VMEM((ROWS,), jnp.int32),
            pltpu.VMEM((ROWS,), jnp.int32),
            pltpu.VMEM((ROWS, KEYS), F32),
            pltpu.VMEM((ROWS, 512), BF16),
            pltpu.VMEM((ROWS, 512), BF16),
            pltpu.VMEM((EXT, 512), BF16),
            pltpu.VMEM((EXT, 1024), BF16),
            pltpu.VMEM((ROWS, 512), BF16),
            pltpu.VMEM((ROWS, D), F32),
            pltpu.VMEM((ROWS, D), BF16),
            pltpu.VMEM((ROWS, D), BF16),
            pltpu.VMEM((ROWS, D), F32),
            pltpu.VMEM((ROWS, 256), BF16),
            pltpu.VMEM((ROWS, 256), BF16),
            dma((7,)),
            dma((PARTS,)),
            dma((PARTS,)),
            dma((PARTS,)),
            dma((2 * PARTS,)),
            dma((2 * PARTS,)),
            dma((2 * PARTS,)),
            dma((2 * PARTS,)),
            dma((6,)),
            dma((6,)),
            dma((CHUNKS + 3,)),
            dma((CHUNKS + 3,)),
        ],
        compiler_params=pltpu.CompilerParams(
            collective_id=0, has_side_effects=True, vmem_limit_bytes=62 << 20
        ),
        cost_estimate=pl.CostEstimate(flops=4_500_000_000, bytes_accessed=4_500_000, transcendentals=1_500_000),
        name="decoder",
    )(state, condition, w_qkv, w_out, time_vector, norm_gain, utterance_ids)


def solution(mesh):
    in_specs = (
        P("seq", None),
        P("seq", None),
        P(),
        P(),
        P(None, None, "mp"),
        P("mp", None),
        P("seq"),
    )
    out_specs = P("seq", "mp")
    return jax.shard_map(shards, mesh=mesh, in_specs=in_specs, out_specs=out_specs, check_vma=False)
```

```python
import jax
import jax.numpy as jnp
from jax import lax
from jax.experimental import pallas as pl
from jax.experimental.pallas import tpu as pltpu
from jax.sharding import PartitionSpec as P

MESH = pl.DeviceIdType.MESH
BF16 = jnp.bfloat16
F32 = jnp.float32

D = 1024
BLOCK = 24
ROWS = 480
EXT = 560
OWN = 48
TILE = 48
KEYS = 128
TILES = ROWS // TILE
LANES = 640
CHUNKS = ((ROWS - 48, 48), (0, 48)) + tuple((r, 96) for r in range(48, ROWS - 48, 96))
PARTS = 8


def kernel(
    state_h, cond_h, wqkv_h, wout_h, tvec_h, gain_h, ids_h, out,
    st, cd, wq, wo, fq, fo, tvec, gain, ids, n1, n2, h1, h2, ids_prev, ids_next, bias, qa, qb, k, v, att, acc,
    pv_out, pv_in, x2, fin_out, fin_in,
    load_sem, zs, zf, zr, xs, xr, ys, yr, hs, hr, ds, dr,
):
    seq = lax.axis_index("seq")
    mp = lax.axis_index("mp")
    x = seq % 4
    y = seq // 16
    odd = y % 2
    zh = mp // 2
    core = mp % 2
    colour = (x + 2 * odd) % 4

    zl = (seq // 4) % 4
    up = (jnp.where(zl == 3, seq - 12, seq + 4), jnp.where(zl == 3, 1 - zh, zh) * 2 + core)
    down = (jnp.where(zl == 0, seq + 12, seq - 4), jnp.where(zl == 0, 1 - zh, zh) * 2 + core)
    outer = (zl == 0) | (zl == 3)
    across = [jnp.where(zl == 3, a, b) for a, b in zip(up, down)]
    inward = [jnp.where(zl == 3, b, a) for a, b in zip(up, down)]
    at_x = [(seq - x + (x + hop) % 4, mp) for hop in (1, 3)]
    at_y = [((seq + 16 * hop) % 128, mp) for hop in (1, 7)]
    before = ((seq + 127) % 128, mp)
    after = ((seq + 1) % 128, mp)
    twin = (seq, zh * 2 + 1 - core)

    barrier = pltpu.get_barrier_semaphore()
    partners = [up, down] + at_x + at_y + [twin]
    for device in partners:
        pl.semaphore_signal(barrier, inc=1, device_id=device, device_id_type=MESH)

    has_before = seq > 0
    has_after = seq < 127

    @pl.when(has_before)
    def _():
        pl.semaphore_signal(barrier, inc=1, device_id=before, device_id_type=MESH)

    @pl.when(has_after)
    def _():
        pl.semaphore_signal(barrier, inc=1, device_id=after, device_id_type=MESH)

    loads = [
        pltpu.make_async_copy(src, dst, load_sem.at[i])
        for i, (src, dst) in enumerate(
            (
                (gain_h, gain),
                (state_h, st),
                (cond_h, cd),
                (ids_h, ids),
                (wqkv_h, wq),
                (wout_h, wo),
                (tvec_h, tvec),
            )
        )
    ]
    for load in loads:
        load.start()

    def remote(src, dst, send, recv, device):
        return pltpu.make_async_remote_copy(
            src_ref=src, dst_ref=dst, send_sem=send, recv_sem=recv, device_id=device, device_id_type=MESH
        )

    def piece(pair, s, which, half=None):
        size, ref = (128, pair[0].at[s // 2]) if s < 6 else (32, pair[1])
        first = 4 * size * (s % 2) + size * which
        if half is not None:
            size = size // 2
            first = first + size * half
        return ref.at[pl.ds(pl.multiple_of(first, 16), size)]

    mine, foreign = (wqkv_h, wout_h), (fq, fo)

    def z_copy(s):
        return remote(piece(mine, s, colour), piece(foreign, s, colour), zs.at[s], zr.at[s], across)

    def z_forward(s):
        return remote(piece(foreign, s, colour), piece(foreign, s, colour), zf.at[s], zr.at[s], inward)

    def x_copy(s, j, which):
        i = 2 * s + j
        return remote(piece(foreign, s, which), piece(foreign, s, which), xs.at[i], xr.at[i], at_x[j])

    def y_copy(s, j, which):
        i = 2 * s + j
        return remote(piece(foreign, s, which, j), piece(foreign, s, which, j), ys.at[i], yr.at[i], at_y[j])

    def tick(s):
        z_copy(s).wait_recv()

        @pl.when(outer)
        def _():
            z_forward(s).start()

        for j in range(2):
            x_copy(s, j, colour).start()
            y_copy(s, j, colour).start()

    def complete(s):
        for j in range(2):
            x_copy(s, j, (colour + 3 - 2 * j) % 4).wait_recv()
            y_copy(s, j, (colour + 2) % 4).wait_recv()

    def halo_copies(n, h, base):
        return (
            remote(n.at[pl.ds(ROWS - 48, 48)], h.at[pl.ds(0, 48)], hs.at[base], hr.at[base], after),
            remote(n.at[pl.ds(0, 32)], h.at[pl.ds(48, 32)], hs.at[base + 1], hr.at[base + 1], before),
        )

    id_copies = (
        remote(ids, ids_prev, hs.at[4], hr.at[4], after),
        remote(ids, ids_next, hs.at[5], hr.at[5], before),
    )

    def send_after(copies):
        @pl.when(has_after)
        def _():
            for copy in copies:
                copy.start()

    def send_before(copies):
        @pl.when(has_before)
        def _():
            for copy in copies:
                copy.start()

    def halo_arrived(copies):
        @pl.when(has_before)
        def _():
            for copy in copies[::2]:
                copy.wait_recv()

        @pl.when(has_after)
        def _():
            for copy in copies[1::2]:
                copy.wait_recv()

    def halo_left(copies):
        @pl.when(has_after)
        def _():
            for copy in copies[::2]:
                copy.wait_send()

        @pl.when(has_before)
        def _():
            for copy in copies[1::2]:
                copy.wait_send()

    def normalise(h, n, r0, rows):
        scale = lax.rsqrt(jnp.mean(h * h, axis=1, keepdims=True) + 1e-06)
        n[pl.ds(r0, rows), :] = (h * scale * gain[...].reshape(1, D).astype(F32)).astype(BF16)

    pl.semaphore_wait(barrier, len(partners) + jnp.where(has_before & has_after, 2, 1))

    @pl.when(outer)
    def _():
        for s in range(PARTS):
            z_copy(s).start()

    for load in loads[:4]:
        load.wait()

    def first_norm(i, _):
        r0 = pl.multiple_of(i * 48, 48)
        h = st[pl.ds(r0, 48), :].astype(F32) + cd[pl.ds(r0, 48), :].astype(F32)
        normalise(h, n1, r0, 48)
        return 0

    lax.fori_loop(0, ROWS // 48, first_norm, 0)
    first_halo = halo_copies(n1, h1, 0)
    send_after((first_halo[0], id_copies[0]))
    send_before((first_halo[1], id_copies[1]))

    @pl.when(seq == 0)
    def _():
        for h in (h1, h2):
            h[0:48, :] = jnp.zeros((48, D), BF16)

    @pl.when(seq == 127)
    def _():
        for h in (h1, h2):
            h[48:80, :] = jnp.zeros((32, D), BF16)

    for load in loads[4:]:
        load.wait()

    for p in range(4):
        v[:, 256 * p + 128 : 256 * p + 256] = jnp.ones((EXT, 128), BF16)

    low = lax.broadcasted_iota(jnp.int32, (1, 128), 1) < 64

    def queries(n, w, pair):
        r = jnp.dot(n[...], w[0], preferred_element_type=F32) * 0.125
        zero = jnp.zeros((), BF16)
        for j in range(2):
            c = 128 * (pair + j)
            part_q = r[:, 128 * j : 128 * j + 128].astype(BF16)
            qa[:, c : c + 128] = jnp.where(low, part_q, zero)
            qb[:, c : c + 128] = jnp.where(low, zero, part_q)

    def spans(halo):
        return ((0, 0, 48), (48, OWN + ROWS, 32)) if halo else ((0, OWN, ROWS),)

    def keys(n, w, pair, halo=False):
        r = jnp.dot(n[...], w[1], preferred_element_type=F32).astype(BF16)
        for r0, to, rows in spans(halo):
            k[to : to + rows, 128 * pair : 128 * pair + 256] = r[r0 : r0 + rows]

    def values(n, w, pair, halo=False):
        r = jnp.dot(n[...], w[2], preferred_element_type=F32).astype(BF16)
        for r0, to, rows in spans(halo):
            for j in range(2):
                c = 256 * (pair + j)
                v[to : to + rows, c : c + 128] = r[r0 : r0 + rows, 128 * j : 128 * j + 128]

    def build_bias():
        lane = lax.broadcasted_iota(jnp.int32, (8, LANES), 1)

        def wide(ref):
            flat = ref[...].astype(F32).reshape(1, ROWS)
            flat = jnp.concatenate([flat, jnp.zeros((1, LANES - ROWS), F32)], axis=1)
            return jnp.broadcast_to(flat, (8, LANES))

        ext = jnp.where(
            lane < OWN,
            jnp.where(seq == 0, -1.0, pltpu.roll(wide(ids_prev), LANES - (ROWS - 48), 1)),
            jnp.where(
                lane < OWN + ROWS,
                pltpu.roll(wide(ids), OWN, 1),
                jnp.where(seq == 127, -2.0, pltpu.roll(wide(ids_next), OWN + ROWS, 1)),
            ),
        )
        row = lax.broadcasted_iota(jnp.int32, (TILE, KEYS), 0)
        col = lax.broadcasted_iota(jnp.int32, (TILE, KEYS), 1)
        first = jnp.where(row < BLOCK, 0, BLOCK)
        window = (col >= first) & (col < first + 4 * BLOCK)
        for t in range(TILES):
            moved = ext if t == 0 else pltpu.roll(ext, LANES - TILE * t, 1)
            key_ids = jnp.broadcast_to(moved[0:1, :KEYS], (TILE, KEYS))
            query_ids = jnp.sum(jnp.where(col == row + OWN, key_ids, 0.0), axis=1, keepdims=True)
            bias[TILE * t : TILE * t + TILE, :] = jnp.where(window & (query_ids == key_ids), 0.0, -1e30)

    def attend(starts, pairs):
        scores = []
        for r0 in starts:
            b = bias[pl.ds(r0, TILE), :]
            b2 = jnp.concatenate([b, b], axis=0)
            for p in pairs:
                c = 128 * p
                q2 = jnp.concatenate([qa[pl.ds(r0, TILE), c : c + 128], qb[pl.ds(r0, TILE), c : c + 128]], axis=0)
                scores.append(
                    lax.dot_general(
                        q2, k[pl.ds(r0, KEYS), c : c + 128], (((1,), (1,)), ((), ())), preferred_element_type=F32
                    )
                    + b2
                )
        tops = [jnp.max(score, axis=1, keepdims=True) for score in scores]
        exps = [jnp.exp(score - top).astype(BF16) for score, top in zip(scores, tops)]
        where = [(r0, 128 * p) for r0 in starts for p in pairs]
        sums = [
            jnp.dot(e, v[pl.ds(r0, KEYS), 2 * c : 2 * c + 256], preferred_element_type=F32)
            for e, (r0, c) in zip(exps, where)
        ]
        for o, (r0, c) in zip(sums, where):
            num = jnp.where(low, o[:TILE, :128], o[TILE:, :128])
            den = jnp.where(low, o[:TILE, 128:], o[TILE:, 128:])
            att[pl.ds(r0, TILE), c : c + 128] = (num / den).astype(BF16)

    def attend_some(start, count, groups, pairs):
        def body(i, _):
            attend([pl.multiple_of((start + count * i + j) * TILE, TILE) for j in range(count)], pairs)
            return 0

        lax.fori_loop(0, groups, body, 0)

    queries(n1, wq, 0)
    tick(0)
    keys(n1, wq, 0)
    tick(1)
    values(n1, wq, 0)
    tick(2)
    tick(3)
    tick(4)
    halo_arrived(first_halo + id_copies)
    keys(h1, wq, 0, True)
    values(h1, wq, 0, True)
    build_bias()
    tick(5)
    attend_some(0, 5, 1, (0, 1))
    tick(6)
    attend_some(5, 5, 1, (0, 1))
    tick(7)
    complete(0)
    complete(1)
    queries(n1, fq, 2)
    for c in range(0, D, 512):
        acc[:, c : c + 512] = jnp.dot(att[:, :256], wo[:, c : c + 512], preferred_element_type=F32)
    complete(2)
    complete(3)
    keys(n1, fq, 2)
    keys(h1, fq, 2, True)
    complete(4)
    complete(5)
    values(n1, fq, 2)
    values(h1, fq, 2, True)
    attend_some(0, 5, 2, (2, 3))
    complete(6)
    complete(7)

    def pv_copy(i):
        span = pl.ds(*CHUNKS[i])
        return remote(pv_out.at[span], pv_in.at[span], ds.at[i], dr.at[i], twin)

    for i, (r0, rows) in enumerate(CHUNKS):
        span = slice(r0, r0 + rows)
        total = acc[span, :] + jnp.dot(att[span, 256:512], fo[...], preferred_element_type=F32)
        acc[span, :] = total
        pv_out[span, :] = total.astype(BF16)
        pv_copy(i).start()

    second_halo = halo_copies(n2, h2, 2)
    for i, (start, rows) in enumerate(CHUNKS):
        pv_copy(i).wait_recv()
        for r0 in range(start, start + rows, 48):
            span = slice(r0, r0 + 48)
            x_new = st[span, :].astype(F32) + 0.5 * (acc[span, :] + pv_in[span, :].astype(F32))
            h = x_new + cd[span, :].astype(F32) + 0.5 * tvec[...].reshape(1, D).astype(F32)
            normalise(h, n2, r0, 48)
        if i == 0:
            send_after(second_halo[:1])
        if i == 1:
            send_before(second_halo[1:])

    queries(n2, wq, 0)
    keys(n2, wq, 0)
    values(n2, wq, 0)
    queries(n2, fq, 2)
    keys(n2, fq, 2)
    attend([TILE * t for t in range(1, 9)], (0, 1))
    values(n2, fq, 2)

    my_cols = pl.ds(pl.multiple_of(512 * zh + 256 * core, 256), 256)
    twin_cols = pl.ds(pl.multiple_of(512 * zh + 256 * (1 - core), 256), 256)

    def terms(r0, rows, cols):
        a = att[r0 : r0 + rows, :]
        return jnp.dot(a[:, :256], wo[:, cols], preferred_element_type=F32) + jnp.dot(
            a[:, 256:512], fo[:, cols], preferred_element_type=F32
        )

    INNER, FIRST, LAST = (TILE, ROWS - 2 * TILE), (0, TILE), (ROWS - TILE, TILE)

    def fin_copy(i, r0, rows):
        span = pl.ds(r0, rows)
        return remote(fin_out.at[span], fin_in.at[span], ds.at[len(CHUNKS) + i], dr.at[len(CHUNKS) + i], twin)

    def send_terms(i, r0, rows):
        fin_out[r0 : r0 + rows, :] = terms(r0, rows, twin_cols).astype(BF16)
        fin_copy(i, r0, rows).start()

    def finish(i, r0, rows):
        fin_copy(i, r0, rows).wait_recv()
        span = slice(r0, r0 + rows)
        out[span, :] = (x2[span, :] + 0.5 * fin_in[span, :].astype(F32)).astype(BF16)

    def own_terms(r0, rows):
        span = slice(r0, r0 + rows)
        x_new = st[span, my_cols].astype(F32) + 0.5 * (acc[span, my_cols] + pv_in[span, my_cols].astype(F32))
        x2[span, :] = x_new + 0.5 * terms(r0, rows, my_cols)

    attend([TILE * t for t in range(1, 9)], (2, 3))
    send_terms(0, *INNER)
    own_terms(*INNER)
    for s in range(PARTS):


        @pl.when(outer)
        def _():
            z_copy(s).wait_send()
            z_forward(s).wait_send()

        for j in range(2):
            x_copy(s, j, colour).wait_send()
            y_copy(s, j, colour).wait_send()
    halo_left(first_halo + id_copies)
    for i in range(len(CHUNKS)):
        pv_copy(i).wait_send()
    halo_arrived(second_halo)
    for w, pair in ((wq, 0), (fq, 2)):
        keys(h2, w, pair, True)
        values(h2, w, pair, True)
    attend((0, (TILES - 1) * TILE), range(4))
    send_terms(1, *FIRST)
    send_terms(2, *LAST)
    finish(0, *INNER)
    own_terms(*FIRST)
    own_terms(*LAST)
    finish(1, *FIRST)
    finish(2, *LAST)

    halo_left(second_halo)
    for i, span in enumerate((INNER, FIRST, LAST)):
        fin_copy(i, *span).wait_send()


def shards(state, condition, time_vector, norm_gain, w_qkv, w_out, utterance_ids):
    any_spec = pl.BlockSpec(memory_space=pl.ANY)
    vmem = pl.BlockSpec(memory_space=pltpu.VMEM)
    dma = pltpu.SemaphoreType.DMA
    return pl.pallas_call(
        kernel,
        out_shape=jax.ShapeDtypeStruct((ROWS, 256), BF16),
        in_specs=[any_spec] * 7,
        out_specs=vmem,
        scratch_shapes=[
            pltpu.VMEM((ROWS, D), BF16),
            pltpu.VMEM((ROWS, D), BF16),
            pltpu.VMEM((3, D, 256), BF16),
            pltpu.VMEM((256, D), BF16),
            pltpu.VMEM((3, D, 256), BF16),
            pltpu.VMEM((256, D), BF16),
            pltpu.VMEM((D,), BF16),
            pltpu.VMEM((D,), BF16),
            pltpu.VMEM((ROWS,), jnp.int32),
            pltpu.VMEM((ROWS, D), BF16),
            pltpu.VMEM((ROWS, D), BF16),
            pltpu.VMEM((80, D), BF16),
            pltpu.VMEM((80, D), BF16),
            pltpu.VMEM((ROWS,), jnp.int32),
            pltpu.VMEM((ROWS,), jnp.int32),
            pltpu.VMEM((ROWS, KEYS), F32),
            pltpu.VMEM((ROWS, 512), BF16),
            pltpu.VMEM((ROWS, 512), BF16),
            pltpu.VMEM((EXT, 512), BF16),
            pltpu.VMEM((EXT, 1024), BF16),
            pltpu.VMEM((ROWS, 512), BF16),
            pltpu.VMEM((ROWS, D), F32),
            pltpu.VMEM((ROWS, D), BF16),
            pltpu.VMEM((ROWS, D), BF16),
            pltpu.VMEM((ROWS, 256), F32),
            pltpu.VMEM((ROWS, 256), BF16),
            pltpu.VMEM((ROWS, 256), BF16),
            dma((7,)),
            dma((PARTS,)),
            dma((PARTS,)),
            dma((PARTS,)),
            dma((2 * PARTS,)),
            dma((2 * PARTS,)),
            dma((2 * PARTS,)),
            dma((2 * PARTS,)),
            dma((6,)),
            dma((6,)),
            dma((len(CHUNKS) + 3,)),
            dma((len(CHUNKS) + 3,)),
        ],
        compiler_params=pltpu.CompilerParams(
            collective_id=0, has_side_effects=True, vmem_limit_bytes=62 << 20
        ),
        cost_estimate=pl.CostEstimate(flops=4_500_000_000, bytes_accessed=4_500_000, transcendentals=1_500_000),
        name="decoder",
    )(state, condition, w_qkv, w_out, time_vector, norm_gain, utterance_ids)


def solution(mesh):
    in_specs = (
        P("seq", None),
        P("seq", None),
        P(),
        P(),
        P(None, None, "mp"),
        P("mp", None),
        P("seq"),
    )
    out_specs = P("seq", "mp")
    return jax.shard_map(shards, mesh=mesh, in_specs=in_specs, out_specs=out_specs, check_vma=False)
```

```python
import jax
import jax.numpy as jnp
from jax import lax
from jax.experimental import pallas as pl
from jax.experimental.pallas import tpu as pltpu
from jax.sharding import PartitionSpec as P

MESH = pl.DeviceIdType.MESH
BF16 = jnp.bfloat16
F32 = jnp.float32

D = 1024
BLOCK = 24
ROWS = 480
EXT = 560
OWN = 48
TILE = 48
KEYS = 128
TILES = ROWS // TILE
LANES = 640
CHUNKS = ((ROWS - 48, 48), (0, 48)) + tuple((r, 192) for r in range(48, ROWS - 48, 192))
PARTS = 8


def kernel(
    state_h, cond_h, wqkv_h, wout_h, tvec_h, gain_h, ids_h, out,
    st, cd, wq, wo, fq, fo, tvec, gain, ids, n1, n2, h1, h2, ids_prev, ids_next, bias, qa, qb, k, v, att, acc,
    pv_out, pv_in, x2, fin_out, fin_in,
    load_sem, zs, zf, zr, xs, xr, ys, yr, hs, hr, ds, dr,
):
    seq = lax.axis_index("seq")
    mp = lax.axis_index("mp")
    x = seq % 4
    y = seq // 16
    odd = y % 2
    zh = mp // 2
    core = mp % 2
    colour = (x + 2 * odd) % 4

    zl = (seq // 4) % 4
    up = (jnp.where(zl == 3, seq - 12, seq + 4), jnp.where(zl == 3, 1 - zh, zh) * 2 + core)
    down = (jnp.where(zl == 0, seq + 12, seq - 4), jnp.where(zl == 0, 1 - zh, zh) * 2 + core)
    outer = (zl == 0) | (zl == 3)
    across = [jnp.where(zl == 3, a, b) for a, b in zip(up, down)]
    inward = [jnp.where(zl == 3, b, a) for a, b in zip(up, down)]
    at_x = [(seq - x + (x + hop) % 4, mp) for hop in (1, 3)]
    at_y = [((seq + 16 * hop) % 128, mp) for hop in (1, 7)]
    before = ((seq + 127) % 128, mp)
    after = ((seq + 1) % 128, mp)
    twin = (seq, zh * 2 + 1 - core)

    barrier = pltpu.get_barrier_semaphore()
    partners = [up, down] + at_x + at_y + [twin]
    for device in partners:
        pl.semaphore_signal(barrier, inc=1, device_id=device, device_id_type=MESH)

    has_before = seq > 0
    has_after = seq < 127

    @pl.when(has_before)
    def _():
        pl.semaphore_signal(barrier, inc=1, device_id=before, device_id_type=MESH)

    @pl.when(has_after)
    def _():
        pl.semaphore_signal(barrier, inc=1, device_id=after, device_id_type=MESH)

    loads = [
        pltpu.make_async_copy(src, dst, load_sem.at[i])
        for i, (src, dst) in enumerate(
            (
                (gain_h, gain),
                (state_h, st),
                (cond_h, cd),
                (ids_h, ids),
                (wqkv_h, wq),
                (wout_h, wo),
                (tvec_h, tvec),
            )
        )
    ]
    for load in loads:
        load.start()

    def remote(src, dst, send, recv, device):
        return pltpu.make_async_remote_copy(
            src_ref=src, dst_ref=dst, send_sem=send, recv_sem=recv, device_id=device, device_id_type=MESH
        )

    def piece(pair, s, which, half=None):
        size, ref = (128, pair[0].at[s // 2]) if s < 6 else (32, pair[1])
        first = 4 * size * (s % 2) + size * which
        if half is not None:
            size = size // 2
            first = first + size * half
        return ref.at[pl.ds(pl.multiple_of(first, 16), size)]

    mine, foreign = (wqkv_h, wout_h), (fq, fo)

    def z_copy(s):
        return remote(piece(mine, s, colour), piece(foreign, s, colour), zs.at[s], zr.at[s], across)

    def z_forward(s):
        return remote(piece(foreign, s, colour), piece(foreign, s, colour), zf.at[s], zr.at[s], inward)

    def x_copy(s, j, which):
        i = 2 * s + j
        return remote(piece(foreign, s, which), piece(foreign, s, which), xs.at[i], xr.at[i], at_x[j])

    def y_copy(s, j, which):
        i = 2 * s + j
        return remote(piece(foreign, s, which, j), piece(foreign, s, which, j), ys.at[i], yr.at[i], at_y[j])

    def tick(s):
        z_copy(s).wait_recv()

        @pl.when(outer)
        def _():
            z_forward(s).start()

        for j in range(2):
            x_copy(s, j, colour).start()
            y_copy(s, j, colour).start()

    def complete(s):
        for j in range(2):
            x_copy(s, j, (colour + 3 - 2 * j) % 4).wait_recv()
            y_copy(s, j, (colour + 2) % 4).wait_recv()

    def halo_copies(n, h, base):
        return (
            remote(n.at[pl.ds(ROWS - 48, 48)], h.at[pl.ds(0, 48)], hs.at[base], hr.at[base], after),
            remote(n.at[pl.ds(0, 32)], h.at[pl.ds(48, 32)], hs.at[base + 1], hr.at[base + 1], before),
        )

    id_copies = (
        remote(ids, ids_prev, hs.at[4], hr.at[4], after),
        remote(ids, ids_next, hs.at[5], hr.at[5], before),
    )

    def send_after(copies):
        @pl.when(has_after)
        def _():
            for copy in copies:
                copy.start()

    def send_before(copies):
        @pl.when(has_before)
        def _():
            for copy in copies:
                copy.start()

    def halo_arrived(copies):
        @pl.when(has_before)
        def _():
            for copy in copies[::2]:
                copy.wait_recv()

        @pl.when(has_after)
        def _():
            for copy in copies[1::2]:
                copy.wait_recv()

    def halo_left(copies):
        @pl.when(has_after)
        def _():
            for copy in copies[::2]:
                copy.wait_send()

        @pl.when(has_before)
        def _():
            for copy in copies[1::2]:
                copy.wait_send()

    def normalise(h, n, r0, rows):
        scale = lax.rsqrt(jnp.mean(h * h, axis=1, keepdims=True) + 1e-06)
        n[pl.ds(r0, rows), :] = (h * scale * gain[...].reshape(1, D).astype(F32)).astype(BF16)

    pl.semaphore_wait(barrier, len(partners) + jnp.where(has_before & has_after, 2, 1))

    @pl.when(outer)
    def _():
        for s in range(PARTS):
            z_copy(s).start()

    for load in loads[:4]:
        load.wait()

    def first_norm(i, _):
        r0 = pl.multiple_of(i * 48, 48)
        h = st[pl.ds(r0, 48), :].astype(F32) + cd[pl.ds(r0, 48), :].astype(F32)
        normalise(h, n1, r0, 48)
        return 0

    lax.fori_loop(0, ROWS // 48, first_norm, 0)
    first_halo = halo_copies(n1, h1, 0)
    send_after((first_halo[0], id_copies[0]))
    send_before((first_halo[1], id_copies[1]))

    @pl.when(seq == 0)
    def _():
        for h in (h1, h2):
            h[0:48, :] = jnp.zeros((48, D), BF16)

    @pl.when(seq == 127)
    def _():
        for h in (h1, h2):
            h[48:80, :] = jnp.zeros((32, D), BF16)

    for load in loads[4:]:
        load.wait()

    for p in range(4):
        v[:, 256 * p + 128 : 256 * p + 256] = jnp.ones((EXT, 128), BF16)

    low = lax.broadcasted_iota(jnp.int32, (1, 128), 1) < 64

    def queries(n, w, pair):
        r = jnp.dot(n[...], w[0], preferred_element_type=F32) * 0.125
        zero = jnp.zeros((), BF16)
        for j in range(2):
            c = 128 * (pair + j)
            part_q = r[:, 128 * j : 128 * j + 128].astype(BF16)
            qa[:, c : c + 128] = jnp.where(low, part_q, zero)
            qb[:, c : c + 128] = jnp.where(low, zero, part_q)

    def spans(halo):
        return ((0, 0, 48), (48, OWN + ROWS, 32)) if halo else ((0, OWN, ROWS),)

    def keys(n, w, pair, halo=False):
        r = jnp.dot(n[...], w[1], preferred_element_type=F32).astype(BF16)
        for r0, to, rows in spans(halo):
            k[to : to + rows, 128 * pair : 128 * pair + 256] = r[r0 : r0 + rows]

    def values(n, w, pair, halo=False):
        r = jnp.dot(n[...], w[2], preferred_element_type=F32).astype(BF16)
        for r0, to, rows in spans(halo):
            for j in range(2):
                c = 256 * (pair + j)
                v[to : to + rows, c : c + 128] = r[r0 : r0 + rows, 128 * j : 128 * j + 128]

    def build_bias():
        lane = lax.broadcasted_iota(jnp.int32, (8, LANES), 1)

        def wide(ref):
            flat = ref[...].astype(F32).reshape(1, ROWS)
            flat = jnp.concatenate([flat, jnp.zeros((1, LANES - ROWS), F32)], axis=1)
            return jnp.broadcast_to(flat, (8, LANES))

        ext = jnp.where(
            lane < OWN,
            jnp.where(seq == 0, -1.0, pltpu.roll(wide(ids_prev), LANES - (ROWS - 48), 1)),
            jnp.where(
                lane < OWN + ROWS,
                pltpu.roll(wide(ids), OWN, 1),
                jnp.where(seq == 127, -2.0, pltpu.roll(wide(ids_next), OWN + ROWS, 1)),
            ),
        )
        row = lax.broadcasted_iota(jnp.int32, (TILE, KEYS), 0)
        col = lax.broadcasted_iota(jnp.int32, (TILE, KEYS), 1)
        first = jnp.where(row < BLOCK, 0, BLOCK)
        window = (col >= first) & (col < first + 4 * BLOCK)
        for t in range(TILES):
            moved = ext if t == 0 else pltpu.roll(ext, LANES - TILE * t, 1)
            key_ids = jnp.broadcast_to(moved[0:1, :KEYS], (TILE, KEYS))
            query_ids = jnp.sum(jnp.where(col == row + OWN, key_ids, 0.0), axis=1, keepdims=True)
            bias[TILE * t : TILE * t + TILE, :] = jnp.where(window & (query_ids == key_ids), 0.0, -1e30)

    def attend(starts, pairs):
        scores = []
        for r0 in starts:
            b = bias[pl.ds(r0, TILE), :]
            b2 = jnp.concatenate([b, b], axis=0)
            for p in pairs:
                c = 128 * p
                q2 = jnp.concatenate([qa[pl.ds(r0, TILE), c : c + 128], qb[pl.ds(r0, TILE), c : c + 128]], axis=0)
                scores.append(
                    lax.dot_general(
                        q2, k[pl.ds(r0, KEYS), c : c + 128], (((1,), (1,)), ((), ())), preferred_element_type=F32
                    )
                    + b2
                )
        tops = [jnp.max(score, axis=1, keepdims=True) for score in scores]
        exps = [jnp.exp(score - top).astype(BF16) for score, top in zip(scores, tops)]
        where = [(r0, 128 * p) for r0 in starts for p in pairs]
        sums = [
            jnp.dot(e, v[pl.ds(r0, KEYS), 2 * c : 2 * c + 256], preferred_element_type=F32)
            for e, (r0, c) in zip(exps, where)
        ]
        for o, (r0, c) in zip(sums, where):
            num = jnp.where(low, o[:TILE, :128], o[TILE:, :128])
            den = jnp.where(low, o[:TILE, 128:], o[TILE:, 128:])
            att[pl.ds(r0, TILE), c : c + 128] = (num / den).astype(BF16)

    def attend_some(start, count, groups, pairs):
        def body(i, _):
            attend([pl.multiple_of((start + count * i + j) * TILE, TILE) for j in range(count)], pairs)
            return 0

        lax.fori_loop(0, groups, body, 0)

    queries(n1, wq, 0)
    tick(0)
    keys(n1, wq, 0)
    tick(1)
    values(n1, wq, 0)
    tick(2)
    tick(3)
    tick(4)
    halo_arrived(first_halo + id_copies)
    keys(h1, wq, 0, True)
    values(h1, wq, 0, True)
    build_bias()
    tick(5)
    attend_some(0, 5, 1, (0, 1))
    tick(6)
    attend_some(5, 5, 1, (0, 1))
    tick(7)
    complete(0)
    complete(1)
    queries(n1, fq, 2)
    for c in range(0, D, 512):
        acc[:, c : c + 512] = jnp.dot(att[:, :256], wo[:, c : c + 512], preferred_element_type=F32)
    complete(2)
    complete(3)
    keys(n1, fq, 2)
    keys(h1, fq, 2, True)
    complete(4)
    complete(5)
    values(n1, fq, 2)
    values(h1, fq, 2, True)
    attend_some(0, 5, 2, (2, 3))
    complete(6)
    complete(7)

    def pv_copy(i):
        span = pl.ds(*CHUNKS[i])
        return remote(pv_out.at[span], pv_in.at[span], ds.at[i], dr.at[i], twin)

    for i, (r0, rows) in enumerate(CHUNKS):
        span = slice(r0, r0 + rows)
        total = acc[span, :] + jnp.dot(att[span, 256:512], fo[...], preferred_element_type=F32)
        acc[span, :] = total
        pv_out[span, :] = total.astype(BF16)
        pv_copy(i).start()

    second_halo = halo_copies(n2, h2, 2)
    for i, (start, rows) in enumerate(CHUNKS):
        pv_copy(i).wait_recv()
        for r0 in range(start, start + rows, 48):
            span = slice(r0, r0 + 48)
            x_new = st[span, :].astype(F32) + 0.5 * (acc[span, :] + pv_in[span, :].astype(F32))
            h = x_new + cd[span, :].astype(F32) + 0.5 * tvec[...].reshape(1, D).astype(F32)
            normalise(h, n2, r0, 48)
        if i == 0:
            send_after(second_halo[:1])
        if i == 1:
            send_before(second_halo[1:])

    queries(n2, wq, 0)
    keys(n2, wq, 0)
    values(n2, wq, 0)
    queries(n2, fq, 2)
    keys(n2, fq, 2)
    attend([TILE * t for t in range(1, 9)], (0, 1))
    values(n2, fq, 2)

    my_cols = pl.ds(pl.multiple_of(512 * zh + 256 * core, 256), 256)
    twin_cols = pl.ds(pl.multiple_of(512 * zh + 256 * (1 - core), 256), 256)

    def terms(r0, rows, cols):
        a = att[r0 : r0 + rows, :]
        return jnp.dot(a[:, :256], wo[:, cols], preferred_element_type=F32) + jnp.dot(
            a[:, 256:512], fo[:, cols], preferred_element_type=F32
        )

    INNER, FIRST, LAST = (TILE, ROWS - 2 * TILE), (0, TILE), (ROWS - TILE, TILE)

    def fin_copy(i, r0, rows):
        span = pl.ds(r0, rows)
        return remote(fin_out.at[span], fin_in.at[span], ds.at[len(CHUNKS) + i], dr.at[len(CHUNKS) + i], twin)

    def send_terms(i, r0, rows):
        fin_out[r0 : r0 + rows, :] = terms(r0, rows, twin_cols).astype(BF16)
        fin_copy(i, r0, rows).start()

    def finish(i, r0, rows):
        fin_copy(i, r0, rows).wait_recv()
        span = slice(r0, r0 + rows)
        out[span, :] = (x2[span, :] + 0.5 * fin_in[span, :].astype(F32)).astype(BF16)

    def own_terms(r0, rows):
        span = slice(r0, r0 + rows)
        x_new = st[span, my_cols].astype(F32) + 0.5 * (acc[span, my_cols] + pv_in[span, my_cols].astype(F32))
        x2[span, :] = x_new + 0.5 * terms(r0, rows, my_cols)

    attend([TILE * t for t in range(1, 9)], (2, 3))
    send_terms(0, *INNER)
    own_terms(*INNER)
    for s in range(PARTS):


        @pl.when(outer)
        def _():
            z_copy(s).wait_send()
            z_forward(s).wait_send()

        for j in range(2):
            x_copy(s, j, colour).wait_send()
            y_copy(s, j, colour).wait_send()
    halo_left(first_halo + id_copies)
    for i in range(len(CHUNKS)):
        pv_copy(i).wait_send()
    halo_arrived(second_halo)
    for w, pair in ((wq, 0), (fq, 2)):
        keys(h2, w, pair, True)
        values(h2, w, pair, True)
    attend((0, (TILES - 1) * TILE), range(4))
    send_terms(1, *FIRST)
    send_terms(2, *LAST)
    finish(0, *INNER)
    own_terms(*FIRST)
    own_terms(*LAST)
    finish(1, *FIRST)
    finish(2, *LAST)

    halo_left(second_halo)
    for i, span in enumerate((INNER, FIRST, LAST)):
        fin_copy(i, *span).wait_send()


def shards(state, condition, time_vector, norm_gain, w_qkv, w_out, utterance_ids):
    any_spec = pl.BlockSpec(memory_space=pl.ANY)
    vmem = pl.BlockSpec(memory_space=pltpu.VMEM)
    dma = pltpu.SemaphoreType.DMA
    return pl.pallas_call(
        kernel,
        out_shape=jax.ShapeDtypeStruct((ROWS, 256), BF16),
        in_specs=[any_spec] * 7,
        out_specs=vmem,
        scratch_shapes=[
            pltpu.VMEM((ROWS, D), BF16),
            pltpu.VMEM((ROWS, D), BF16),
            pltpu.VMEM((3, D, 256), BF16),
            pltpu.VMEM((256, D), BF16),
            pltpu.VMEM((3, D, 256), BF16),
            pltpu.VMEM((256, D), BF16),
            pltpu.VMEM((D,), BF16),
            pltpu.VMEM((D,), BF16),
            pltpu.VMEM((ROWS,), jnp.int32),
            pltpu.VMEM((ROWS, D), BF16),
            pltpu.VMEM((ROWS, D), BF16),
            pltpu.VMEM((80, D), BF16),
            pltpu.VMEM((80, D), BF16),
            pltpu.VMEM((ROWS,), jnp.int32),
            pltpu.VMEM((ROWS,), jnp.int32),
            pltpu.VMEM((ROWS, KEYS), F32),
            pltpu.VMEM((ROWS, 512), BF16),
            pltpu.VMEM((ROWS, 512), BF16),
            pltpu.VMEM((EXT, 512), BF16),
            pltpu.VMEM((EXT, 1024), BF16),
            pltpu.VMEM((ROWS, 512), BF16),
            pltpu.VMEM((ROWS, D), F32),
            pltpu.VMEM((ROWS, D), BF16),
            pltpu.VMEM((ROWS, D), BF16),
            pltpu.VMEM((ROWS, 256), F32),
            pltpu.VMEM((ROWS, 256), BF16),
            pltpu.VMEM((ROWS, 256), BF16),
            dma((7,)),
            dma((PARTS,)),
            dma((PARTS,)),
            dma((PARTS,)),
            dma((2 * PARTS,)),
            dma((2 * PARTS,)),
            dma((2 * PARTS,)),
            dma((2 * PARTS,)),
            dma((6,)),
            dma((6,)),
            dma((len(CHUNKS) + 3,)),
            dma((len(CHUNKS) + 3,)),
        ],
        compiler_params=pltpu.CompilerParams(
            collective_id=0, has_side_effects=True, vmem_limit_bytes=62 << 20
        ),
        cost_estimate=pl.CostEstimate(flops=4_500_000_000, bytes_accessed=4_500_000, transcendentals=1_500_000),
        name="decoder",
    )(state, condition, w_qkv, w_out, time_vector, norm_gain, utterance_ids)


def solution(mesh):
    in_specs = (
        P("seq", None),
        P("seq", None),
        P(),
        P(),
        P(None, None, "mp"),
        P("mp", None),
        P("seq"),
    )
    out_specs = P("seq", "mp")
    return jax.shard_map(shards, mesh=mesh, in_specs=in_specs, out_specs=out_specs, check_vma=False)
```
